32 devices in a mesh: seq: 8 (over z, y), head: 4 (over x, core).
Axes of the slice: x: 2, y: 2, z: 4, core: 2. Of those that a mesh axis runs over, the one named last changes fastest.
Arguments:
- queries: bfloat16 [2048, 4096], P('seq', 'head'), may hold values from -32 to 32
- key_rows: bfloat16 [2048, 4096], P('seq', 'head'), may hold values from -6 to 6
- value_rows: bfloat16 [2048, 4096], P('seq', 'head'), may hold values from -6 to 6
- out_weight: bfloat16 [4096, 4096], P('head', 'seq'), may hold values from -0.125 to 0.125
- grad_output: bfloat16 [2048, 4096], P('seq', 'head'), may hold values from -6 to 6
- cluster_ids: int32 [2048], P('seq'), may hold values from 0 to 7, as said below
- block_pattern: int32 [8, 2, 2], replicated, may hold values from 0 to 1, as said below
Outputs:
- layer_out: bfloat16 [2048, 4096], P('seq', 'head')
- grad_queries: bfloat16 [2048, 4096], P('seq', 'head')
- grad_keys: bfloat16 [2048, 4096], P('seq', 'head')
- grad_values: bfloat16 [2048, 4096], P('seq', 'head')
The draws below stay inside these ranges and needn't reach their ends.
Inputs may be any that keep to these rules, and one draw needn't show every extreme that they name: `cluster_ids`: every cluster holds exactly 256 tokens. The 256 tokens of one index of seq name one cluster at most 64 times, and each such index names some cluster exactly 64 times. block_pattern[c, b, b] = 1 and block_pattern[c, b, b2] = 0 for b2 > b.
All inputs are finite; a program needn't handle non-finite values.
Results may differ from the reference program's by a relative error of at most 0.03.
Values may be sent and summed in bfloat16 or wider, within the bound.
A program may use at most 64 MiB of HBM per device.

```python
import math
import jax
import jax.numpy as jnp
from jax import lax

D = 4096
H = 32
HD = 128
BLK = 128
TOK_DEV = 256
TOKENS = 2048
CLUSTERS = 8
NB = 2
GROUP_HEADS = 8


def cluster_table(key):
    base = jax.random.fold_in(key, 5)
    key_rise, key_shift, key_order = jax.random.split(base, 3)
    even_share = TOK_DEV // CLUSTERS
    rising = jax.random.randint(key_rise, (CLUSTERS,), 0, even_share + 1)
    rising = rising.at[0].set(even_share).at[CLUSTERS - 1].set(0)
    deviation = rising - jnp.roll(rising, 1)
    shifts = jax.random.permutation(key_shift, CLUSTERS).astype(jnp.int32)
    columns = jnp.arange(CLUSTERS, dtype=jnp.int32)
    counts = even_share + deviation[(columns[None, :] - shifts[:, None]) % CLUSTERS]
    ends = jnp.cumsum(counts, axis=1)
    places = jnp.arange(TOK_DEV, dtype=jnp.int32)
    labels = jnp.sum((ends[:, None, :] <= places[None, :, None]).astype(jnp.int32), axis=2)
    orders = jax.vmap(lambda sub_key: jax.random.permutation(sub_key, TOK_DEV))(jax.random.split(key_order, CLUSTERS))
    mixed = jnp.take_along_axis(labels, orders.astype(jnp.int32), axis=1)
    return mixed


def pair_draw(key):
    base = jax.random.fold_in(key, 9)
    key_query, key_keys = jax.random.split(base, 2)
    query_vals = jnp.clip(jax.random.normal(key_query, (TOKENS, H * HD), jnp.float32), -6.0, 6.0)
    key_vals = jnp.clip(jax.random.normal(key_keys, (TOKENS, H * HD), jnp.float32), -6.0, 6.0)
    return (query_vals, key_vals)


def draw_queries(key, part):
    return pair_draw(key)[0].astype(jnp.bfloat16)


def draw_key_rows(key, part):
    return pair_draw(key)[1].astype(jnp.bfloat16)


def draw_cluster_ids(key, part):
    return cluster_table(key).reshape(TOKENS).astype(jnp.int32)


def draw_block_pattern(key, part):
    base = jax.random.fold_in(key, 13)
    coins = jax.random.randint(base, (CLUSTERS, NB, NB), 0, 2)
    row_block = jnp.arange(NB, dtype=jnp.int32)[:, None]
    col_block = jnp.arange(NB, dtype=jnp.int32)[None, :]
    return jnp.where(row_block == col_block, 1, jnp.where(row_block > col_block, coins, 0)).astype(jnp.int32)


def with_spikes(entries, stream_key, source, target, parts, factor):
    owner, partner = [(jnp.arange(entries.shape[position]) // (entries.shape[position] // parts)).reshape([-1 if axis == position else 1 for axis in range(entries.ndim)]) for position in (source, target)]
    chosen = jax.random.permutation(stream_key, parts)[partner]
    strong = (owner == chosen) | (owner == (partner + parts // 2) % parts)
    return jnp.where(strong, factor * entries, entries)


def levels(rng, extent, cuts, smallest, high):
    loudness = 1.0
    for position, blocks in cuts:
        draws = jax.random.uniform(jax.random.fold_in(jax.random.fold_in(rng, 6), position), (blocks,), jnp.float32, smallest / len(cuts), high / len(cuts))
        loudness = loudness * jnp.repeat(jnp.exp(draws), extent[position] // blocks).reshape((-1,) + (1,) * (len(extent) - 1 - position))
    return loudness


def bell_draw(own_key, shape, scale, limit, cuts=(), held_as=jnp.bfloat16):
    result = jax.random.normal(own_key, shape, jnp.float32) * scale
    if len(cuts) > 0:
        result = levels(own_key, shape, cuts, -0.22, 0.18) * result
    return jnp.clip(result, min=-limit, max=limit).astype(held_as)


def noise_with(key, shape, width, reach, shards, heavy, kind=jnp.bfloat16):
    array = width * jax.random.normal(key, shape, jnp.float32)
    if shards:
        array = array * levels(key, shape, shards, -0.22, 0.18)
    return jnp.clip(with_spikes(array, jax.random.fold_in(key, 3), *heavy), -reach, reach).astype(kind)


def setup_inputs(seed: int = 0) -> dict:
    arg_keys = jax.random.split(jax.random.key(seed), 8)
    queries = draw_queries(jax.random.fold_in(arg_keys[7], 71), 0)
    key_rows = draw_key_rows(jax.random.fold_in(arg_keys[7], 71), 0)
    value_rows = bell_draw(arg_keys[2], (TOKENS, H * HD), 1.0, 6.0, ((0, 8), (1, 4)))
    out_weight = noise_with(arg_keys[3], (H * HD, D), (H * HD) ** -0.5, 0.125, ((0, 4), (1, 8)), (0, 1, 8, 2.0))
    grad_output = bell_draw(arg_keys[4], (TOKENS, D), 1.0, 6.0, ((0, 8), (1, 4)))
    cluster_ids = draw_cluster_ids(jax.random.fold_in(arg_keys[7], 71), 0)
    block_pattern = draw_block_pattern(jax.random.fold_in(arg_keys[7], 71), 0)
    return {"queries": queries, "key_rows": key_rows, "value_rows": value_rows, "out_weight": out_weight, "grad_output": grad_output, "cluster_ids": cluster_ids, "block_pattern": block_pattern}


def reference(queries, key_rows, value_rows, out_weight, grad_output, cluster_ids, block_pattern):
    score_scale = 1.0 / math.sqrt(HD)
    cluster_order = jnp.argsort(cluster_ids, stable=True).astype(jnp.int32).reshape(CLUSTERS, TOK_DEV)
    flat_order = cluster_order.reshape(-1)
    cluster_rank = jnp.arange(TOK_DEV, dtype=jnp.int32)
    block_of = cluster_rank // BLK
    causal = cluster_rank[None, :] <= cluster_rank[:, None]

    def allowed_of(pattern):
        return causal & (pattern[block_of][:, block_of] == 1)

    def split_heads(row_data):
        return row_data.reshape(TOK_DEV, H, HD).astype(jnp.float32)

    def rounded(values):
        return lax.optimization_barrier(values.astype(jnp.bfloat16)).astype(jnp.float32)

    def probabilities(query_heads, key_heads, allowed):
        scores = jnp.einsum('qhd,khd->hqk', query_heads, key_heads) * score_scale
        scores = jnp.where(allowed[None], scores, -jnp.inf)
        shifted = jnp.exp(scores - lax.optimization_barrier(jnp.max(scores, axis=2, keepdims=True)))
        return shifted / lax.optimization_barrier(jnp.sum(shifted, axis=2, keepdims=True))

    def forward_one(operands):
        members, pattern = operands
        probs = probabilities(split_heads(queries[members]), split_heads(key_rows[members]), allowed_of(pattern))
        mixed = jnp.einsum('hqk,khd->qhd', rounded(probs), split_heads(value_rows[members]))
        return mixed.reshape(TOK_DEV, H * HD).astype(jnp.bfloat16)
    per_cluster = lax.map(forward_one, (cluster_order, block_pattern))
    attention = jnp.zeros((TOKENS, H * HD), jnp.bfloat16).at[flat_order].set(per_cluster.reshape(TOKENS, H * HD))
    group_width = GROUP_HEADS * HD
    summed = jnp.zeros((TOKENS, D), jnp.float32)
    for group in range(H // GROUP_HEADS):
        part_cols = attention[:, group * group_width:(group + 1) * group_width]
        part_rows = out_weight[group * group_width:(group + 1) * group_width]
        summed = summed + rounded(jnp.dot(part_cols, part_rows, preferred_element_type=jnp.float32))
    layer_out = summed.astype(jnp.bfloat16)
    grad_attention = jnp.dot(grad_output, out_weight.T, preferred_element_type=jnp.float32).astype(jnp.bfloat16)

    def backward_one(operands):
        members, pattern = operands
        query_heads = split_heads(queries[members])
        key_heads = split_heads(key_rows[members])
        value_heads = split_heads(value_rows[members])
        grad_heads = split_heads(grad_attention[members])
        attn_heads = split_heads(attention[members])
        probs = probabilities(query_heads, key_heads, allowed_of(pattern))
        delta = lax.optimization_barrier(jnp.sum(grad_heads * attn_heads, axis=2)).T[:, :, None]
        dprobs = jnp.einsum('qhd,khd->hqk', grad_heads, value_heads)
        dscores = rounded(probs * (dprobs - delta))
        grad_q = jnp.einsum('hqk,khd->qhd', dscores, key_heads) * score_scale
        grad_k = jnp.einsum('hqk,qhd->khd', dscores, query_heads) * score_scale
        grad_v = jnp.einsum('hqk,qhd->khd', rounded(probs), grad_heads)
        return (grad_q.reshape(TOK_DEV, H * HD).astype(jnp.bfloat16), grad_k.reshape(TOK_DEV, H * HD).astype(jnp.bfloat16), grad_v.reshape(TOK_DEV, H * HD).astype(jnp.bfloat16))
    cluster_q, cluster_k, cluster_v = lax.map(backward_one, (cluster_order, block_pattern))

    def unsort(per_rows):
        return jnp.zeros((TOKENS, H * HD), jnp.bfloat16).at[flat_order].set(per_rows.reshape(TOKENS, H * HD))
    return (layer_out, unsort(cluster_q), unsort(cluster_k), unsort(cluster_v))
```

```python
import functools
import math

import jax
import jax.numpy as jnp
from jax import lax
from jax.experimental import pallas as pl
from jax.experimental.pallas import tpu as pltpu
from jax.sharding import PartitionSpec as P

HD = 128
BLK = 128


def probabilities(query_part, key_part, allowed, score_scale):
    scores = (
        jnp.einsum("qd,kd->qk", query_part, key_part, preferred_element_type=jnp.float32)
        * score_scale
    )
    scores = jnp.where(allowed, scores, -jnp.inf)
    shifted = jnp.exp(scores - jnp.max(scores, axis=1, keepdims=True))
    return shifted / jnp.sum(shifted, axis=1, keepdims=True)


def attend(query_side, key_side, value_side, allowed, head_count, score_scale):
    results = []
    for which_head in range(head_count):
        lower = which_head * HD
        probs = probabilities(
            query_side[:, lower : lower + HD], key_side[:, lower : lower + HD], allowed, score_scale
        )
        mixed = jnp.dot(
            probs.astype(jnp.bfloat16),
            value_side[:, lower : lower + HD],
            preferred_element_type=jnp.float32,
        )
        results.append(mixed.astype(jnp.bfloat16))
    return jnp.concatenate(results, axis=1)


def attend_back(
    query_side, key_side, value_side, allowed, attn_side, grad_side, head_count, score_scale
):
    grad_q, grad_k, grad_v = ([], [], [])
    for which_head in range(head_count):
        lower = which_head * HD
        query_head = query_side[:, lower : lower + HD]
        key_head = key_side[:, lower : lower + HD]
        value_head = value_side[:, lower : lower + HD]
        grad_head = grad_side[:, lower : lower + HD]
        attn_head = attn_side[:, lower : lower + HD]
        probs = probabilities(query_head, key_head, allowed, score_scale)
        probs_low = probs.astype(jnp.bfloat16)
        delta = jnp.sum(
            grad_head.astype(jnp.float32) * attn_head.astype(jnp.float32), axis=1, keepdims=True
        )
        dprobs = jnp.einsum("qd,kd->qk", grad_head, value_head, preferred_element_type=jnp.float32)
        dscores = (probs * (dprobs - delta)).astype(jnp.bfloat16)
        grad_q.append(
            (jnp.dot(dscores, key_head, preferred_element_type=jnp.float32) * score_scale).astype(
                jnp.bfloat16
            )
        )
        grad_k.append(
            (
                jnp.einsum("qk,qd->kd", dscores, query_head, preferred_element_type=jnp.float32)
                * score_scale
            ).astype(jnp.bfloat16)
        )
        grad_v.append(
            jnp.einsum(
                "qk,qd->kd", probs_low, grad_head, preferred_element_type=jnp.float32
            ).astype(jnp.bfloat16)
        )
    return (
        jnp.concatenate(grad_q, axis=1),
        jnp.concatenate(grad_k, axis=1),
        jnp.concatenate(grad_v, axis=1),
    )


def by_clusters(queries, key_rows, value_rows, out_weight, grad_output, cluster_ids, block_pattern):
    tokens = queries.shape[0]
    width = queries.shape[1]
    head_count = width // HD
    groups = lax.axis_size("seq")
    slot_rows = 2 * tokens // groups
    slot_total = groups * slot_rows
    blocks = block_pattern.shape[1]
    owner_index = lax.axis_index("seq")
    score_scale = 1.0 / math.sqrt(HD)
    members = (cluster_ids[:, None] == jnp.arange(groups, dtype=jnp.int32)[None, :]).astype(
        jnp.int32
    )
    earlier = jnp.cumsum(members, axis=0) - members
    local_rank = jnp.sum(earlier * members, axis=1)
    send_counts = jnp.sum(members, axis=0)
    slot_index = cluster_ids * slot_rows + local_rank

    def to_slots(row_data):
        return (
            jnp.zeros((slot_total, row_data.shape[1]), row_data.dtype).at[slot_index].set(row_data)
        )

    def from_slots(buffer):
        return jnp.take(buffer, slot_index, axis=0)

    full_weight = lax.all_gather(out_weight, "seq", axis=1, tiled=True)
    query_in, key_in, value_in, got_counts = (
        lax.all_to_all(to_slots(queries), "seq", split_axis=0, concat_axis=0, tiled=True),
        lax.all_to_all(to_slots(key_rows), "seq", split_axis=0, concat_axis=0, tiled=True),
        lax.all_to_all(to_slots(value_rows), "seq", split_axis=0, concat_axis=0, tiled=True),
        lax.all_to_all(send_counts, "seq", split_axis=0, concat_axis=0, tiled=True),
    )
    offsets = jnp.cumsum(got_counts) - got_counts
    pattern = lax.dynamic_index_in_dim(block_pattern, owner_index, 0, keepdims=False).astype(
        jnp.float32
    )
    slot_source = jnp.arange(slot_total, dtype=jnp.int32) // slot_rows
    slot_place = jnp.arange(slot_total, dtype=jnp.int32) % slot_rows
    row_live = slot_place < jnp.take(got_counts, slot_source)
    rank_rows = jnp.take(offsets, slot_source) + slot_place
    query_side, key_side, value_side = (query_in, key_in, value_in)
    onehot = (rank_rows[:, None] // BLK == jnp.arange(blocks, dtype=jnp.int32)[None, :]).astype(
        jnp.float32
    )
    block_ok = jnp.dot(jnp.dot(onehot, pattern), onehot.T) > 0.5
    usable = (
        block_ok
        & (rank_rows[None, :] <= rank_rows[:, None])
        & row_live[None, :]
        & row_live[:, None]
    )
    diagonal = jnp.eye(rank_rows.shape[0], dtype=bool)
    allowed = usable | diagonal & ~row_live[:, None]
    attn_side = attend(query_side, key_side, value_side, allowed, head_count, score_scale)
    attn_local = from_slots(
        lax.all_to_all(attn_side, "seq", split_axis=0, concat_axis=0, tiled=True)
    )
    partial_value = jnp.dot(attn_local, full_weight, preferred_element_type=jnp.float32)
    rounded_part = lax.optimization_barrier(partial_value.astype(jnp.bfloat16)).astype(jnp.float32)
    layer_out = lax.psum_scatter(
        rounded_part.astype(jnp.bfloat16), "head", scatter_dimension=1, tiled=True
    )
    grad_sum = jnp.einsum(
        "td,wd->tw",
        lax.all_gather(grad_output, "head", axis=1, tiled=True),
        full_weight,
        preferred_element_type=jnp.float32,
    )
    grad_attention = grad_sum.astype(jnp.bfloat16)
    grad_in = lax.all_to_all(
        to_slots(grad_attention), "seq", split_axis=0, concat_axis=0, tiled=True
    )
    grad_q, grad_k, grad_v = attend_back(
        query_side, key_side, value_side, allowed, attn_side, grad_in, head_count, score_scale
    )
    back_q, back_k, back_v = (
        lax.all_to_all(grad_q, "seq", split_axis=0, concat_axis=0, tiled=True),
        lax.all_to_all(grad_k, "seq", split_axis=0, concat_axis=0, tiled=True),
        lax.all_to_all(grad_v, "seq", split_axis=0, concat_axis=0, tiled=True),
    )
    return (layer_out, from_slots(back_q), from_slots(back_k), from_slots(back_v))


ID_ROWS = 16


def one_hot(hit):
    return jnp.where(hit, 1.0, 0.0).astype(jnp.bfloat16)


def dot_rows(left, right):
    return lax.dot_general(
        left, right, (((1,), (0,)), ((), ())), preferred_element_type=jnp.float32
    )


def dot_last(left, right):
    return lax.dot_general(
        left, right, (((1,), (1,)), ((), ())), preferred_element_type=jnp.float32
    )


def dot_first(left, right):
    return lax.dot_general(
        left, right, (((0,), (0,)), ((), ())), preferred_element_type=jnp.float32
    )


def cluster_places(arrived_ref, rows, parts, place_ref, place_cols_ref):
    before = lax.broadcasted_iota(jnp.int32, (rows, rows), 0)
    after = lax.broadcasted_iota(jnp.int32, (rows, rows), 1)
    strict = one_hot(before < after)
    names = lax.broadcasted_iota(jnp.int32, (parts, rows), 0).astype(jnp.float32)
    seen = jnp.zeros((parts, 1), jnp.float32)
    lines = []
    for part in range(parts):
        ids = jnp.concatenate(
            [
                arrived_ref[part, 3 * rows + i : 3 * rows + i + 1, :].astype(jnp.float32)
                for i in range(rows // HD)
            ],
            axis=1,
        )
        hit = names == ids
        mark = jnp.where(hit, 1.0, 0.0)
        rank = dot_rows(mark.astype(jnp.bfloat16), strict) + seen
        lines.append(jnp.sum(mark * (rank + names * rows), axis=0, keepdims=True))
        seen = seen + jnp.sum(mark, axis=1, keepdims=True)
    places = jnp.concatenate(lines, axis=0)
    place_ref[...] = places
    padded = jnp.concatenate([places, jnp.zeros((HD - parts, rows), jnp.float32)], axis=0)
    place_cols_ref[...] = padded.T


def to_cluster(place_ref, rows, parts, cluster, read_part):
    want = lax.broadcasted_iota(jnp.int32, (rows, rows), 0).astype(jnp.float32) + (
        cluster * rows
    ).astype(jnp.float32)
    total = None
    for part in range(parts):
        pick = one_hot(want == place_ref[part : part + 1, :])
        term = dot_rows(pick, read_part(part))
        total = term if total is None else total + term
    return total.astype(jnp.bfloat16)


def from_clusters(place_cols_ref, rows, parts, part, ordered):
    lanes = lax.broadcasted_iota(jnp.int32, (rows, parts * rows), 1).astype(jnp.float32)
    pick = one_hot(place_cols_ref[:, part : part + 1] == lanes)
    return dot_rows(pick, ordered).astype(jnp.bfloat16)


def cluster_probs(pattern_ref, cluster, query, key, rows, score_scale):
    scores = dot_last(query, key) * score_scale
    row_at = lax.broadcasted_iota(jnp.int32, (rows, rows), 0)
    col_at = lax.broadcasted_iota(jnp.int32, (rows, rows), 1)
    reads = pattern_ref[cluster * 4 + 2]
    ok = (col_at <= row_at) & ((row_at // BLK == col_at // BLK) | (reads == 1))
    scores = jnp.where(ok, scores, -jnp.inf)
    shifted = jnp.exp(scores - jnp.max(scores, axis=1, keepdims=True))
    return shifted / jnp.sum(shifted, axis=1, keepdims=True)


def forward_kernel(
    rows, parts, pattern_ref, arrived_ref, mixed_ref, sorted_ref, place_ref, place_cols_ref, held
):
    score_scale = 1.0 / math.sqrt(HD)
    cluster_places(arrived_ref, rows, parts, place_ref, place_cols_ref)

    def step(cluster, _):
        def read_part(part):
            return jnp.concatenate(
                [arrived_ref[part, i * rows : (i + 1) * rows, :] for i in range(3)], axis=1
            )

        picked = to_cluster(place_ref, rows, parts, cluster, read_part)
        sorted_ref[cluster] = picked
        query, key, value = (picked[:, i * HD : (i + 1) * HD] for i in range(3))
        probs = cluster_probs(pattern_ref, cluster, query, key, rows, score_scale)
        at = pl.multiple_of(cluster * rows, rows)
        held[pl.ds(at, rows), :] = dot_rows(probs.astype(jnp.bfloat16), value).astype(jnp.bfloat16)
        return 0

    lax.fori_loop(0, parts, step, 0, unroll=2)
    for part in range(parts):
        mixed_ref[part] = from_clusters(place_cols_ref, rows, parts, part, held[...])


def backward_kernel(
    rows, parts, pattern_ref, sorted_ref, place_ref, place_cols_ref, grad_ref, out_ref, held
):
    score_scale = 1.0 / math.sqrt(HD)

    def step(cluster, _):
        grad = to_cluster(place_ref, rows, parts, cluster, lambda part: grad_ref[part])
        picked = sorted_ref[cluster]
        query, key, value = (picked[:, i * HD : (i + 1) * HD] for i in range(3))
        probs = cluster_probs(pattern_ref, cluster, query, key, rows, score_scale)
        low = probs.astype(jnp.bfloat16)
        mixed = dot_rows(low, value).astype(jnp.bfloat16).astype(jnp.float32)
        delta = jnp.sum(grad.astype(jnp.float32) * mixed, axis=1, keepdims=True)
        dscores = (probs * (dot_last(grad, value) - delta)).astype(jnp.bfloat16)
        at = pl.multiple_of(cluster * rows, rows)
        here = pl.ds(at, rows)
        held[here, 0:HD] = (dot_rows(dscores, key) * score_scale).astype(jnp.bfloat16)
        held[here, HD : 2 * HD] = (dot_first(dscores, query) * score_scale).astype(jnp.bfloat16)
        held[here, 2 * HD : 3 * HD] = dot_first(low, grad).astype(jnp.bfloat16)
        return 0

    lax.fori_loop(0, parts, step, 0, unroll=2)
    for part in range(parts):
        back = from_clusters(place_cols_ref, rows, parts, part, held[...])
        for i in range(3):
            out_ref[part, i * rows : (i + 1) * rows, :] = back[:, i * HD : (i + 1) * HD]


VMEM_SPEC = pl.BlockSpec(memory_space=pltpu.VMEM)
SMEM_SPEC = pl.BlockSpec(memory_space=pltpu.SMEM)
PARAMS = pltpu.CompilerParams(vmem_limit_bytes=48 * 1024 * 1024)


def by_heads(queries, key_rows, value_rows, out_weight, grad_output, cluster_ids, block_pattern):
    rows, width = queries.shape
    parts = lax.axis_size("seq")
    pattern = block_pattern.reshape(-1)

    def heads_first(row_data):
        return row_data.reshape(rows, parts, HD).transpose(1, 0, 2)

    def heads_last(row_data):
        return row_data.transpose(1, 0, 2).reshape(rows, width)

    def swap(buffer):
        return lax.all_to_all(buffer, "seq", split_axis=0, concat_axis=0, tiled=True)

    id_rows = jnp.zeros((ID_ROWS, HD), jnp.bfloat16)
    id_rows = id_rows.at[: rows // HD].set(cluster_ids.reshape(-1, HD).astype(jnp.bfloat16))
    id_rows = jnp.broadcast_to(id_rows[None], (parts, ID_ROWS, HD))
    packed = jnp.concatenate(
        [heads_first(queries), heads_first(key_rows), heads_first(value_rows), id_rows], axis=1
    )
    full_weight = lax.all_gather(out_weight, "seq", axis=1, tiled=True)
    full_grad = lax.all_gather(grad_output, "head", axis=1, tiled=True)
    arrived = swap(packed)
    mixed, ordered, places, place_cols = pl.pallas_call(
        functools.partial(forward_kernel, rows, parts),
        out_shape=(
            jax.ShapeDtypeStruct((parts, rows, HD), jnp.bfloat16),
            jax.ShapeDtypeStruct((parts, rows, 3 * HD), jnp.bfloat16),
            jax.ShapeDtypeStruct((parts, rows), jnp.float32),
            jax.ShapeDtypeStruct((rows, HD), jnp.float32),
        ),
        in_specs=[SMEM_SPEC, VMEM_SPEC],
        out_specs=(VMEM_SPEC,) * 4,
        scratch_shapes=[pltpu.VMEM((parts * rows, HD), jnp.bfloat16)],
        compiler_params=PARAMS,
        name="attention_forward",
    )(pattern, arrived)
    attn_local = heads_last(swap(mixed))
    grad_attention = jnp.einsum(
        "td,wd->tw", full_grad, full_weight, preferred_element_type=jnp.float32
    ).astype(jnp.bfloat16)
    grad_in = swap(heads_first(grad_attention))
    grads = pl.pallas_call(
        functools.partial(backward_kernel, rows, parts),
        out_shape=jax.ShapeDtypeStruct((parts, 3 * rows, HD), jnp.bfloat16),
        in_specs=[SMEM_SPEC] + [VMEM_SPEC] * 4,
        out_specs=VMEM_SPEC,
        scratch_shapes=[pltpu.VMEM((parts * rows, 3 * HD), jnp.bfloat16)],
        compiler_params=PARAMS,
        name="attention_backward",
    )(pattern, ordered, places, place_cols, grad_in)
    partial_value = jnp.dot(attn_local, full_weight, preferred_element_type=jnp.float32)
    layer_out = lax.psum_scatter(
        partial_value.astype(jnp.bfloat16), "head", scatter_dimension=1, tiled=True
    )
    back = swap(grads)
    return (layer_out,) + tuple(heads_last(back[:, i * rows : (i + 1) * rows]) for i in range(3))


def on_device(queries, *others):
    heads = queries.shape[1] // HD
    if heads == lax.axis_size("seq") and others[-1].shape[1] == 2:
        return by_heads(queries, *others)
    return by_clusters(queries, *others)


def solution(mesh):
    in_specs = (
        P("seq", "head"),
        P("seq", "head"),
        P("seq", "head"),
        P("head", "seq"),
        P("seq", "head"),
        P("seq"),
        P(),
    )
    out_specs = (P("seq", "head"), P("seq", "head"), P("seq", "head"), P("seq", "head"))
    return jax.shard_map(
        on_device, mesh=mesh, in_specs=in_specs, out_specs=out_specs, check_vma=False
    )
```

```python
import functools
import math

import jax
import jax.numpy as jnp
from jax import lax
from jax.experimental import pallas as pl
from jax.experimental.pallas import tpu as pltpu
from jax.sharding import PartitionSpec as P

HD = 128
BLK = 128


def probabilities(query_part, key_part, allowed, score_scale):
    scores = (
        jnp.einsum("qd,kd->qk", query_part, key_part, preferred_element_type=jnp.float32)
        * score_scale
    )
    scores = jnp.where(allowed, scores, -jnp.inf)
    shifted = jnp.exp(scores - jnp.max(scores, axis=1, keepdims=True))
    return shifted / jnp.sum(shifted, axis=1, keepdims=True)


def attend(query_side, key_side, value_side, allowed, head_count, score_scale):
    results = []
    for which_head in range(head_count):
        lower = which_head * HD
        probs = probabilities(
            query_side[:, lower : lower + HD], key_side[:, lower : lower + HD], allowed, score_scale
        )
        mixed = jnp.dot(
            probs.astype(jnp.bfloat16),
            value_side[:, lower : lower + HD],
            preferred_element_type=jnp.float32,
        )
        results.append(mixed.astype(jnp.bfloat16))
    return jnp.concatenate(results, axis=1)


def attend_back(
    query_side, key_side, value_side, allowed, attn_side, grad_side, head_count, score_scale
):
    grad_q, grad_k, grad_v = ([], [], [])
    for which_head in range(head_count):
        lower = which_head * HD
        query_head = query_side[:, lower : lower + HD]
        key_head = key_side[:, lower : lower + HD]
        value_head = value_side[:, lower : lower + HD]
        grad_head = grad_side[:, lower : lower + HD]
        attn_head = attn_side[:, lower : lower + HD]
        probs = probabilities(query_head, key_head, allowed, score_scale)
        probs_low = probs.astype(jnp.bfloat16)
        delta = jnp.sum(
            grad_head.astype(jnp.float32) * attn_head.astype(jnp.float32), axis=1, keepdims=True
        )
        dprobs = jnp.einsum("qd,kd->qk", grad_head, value_head, preferred_element_type=jnp.float32)
        dscores = (probs * (dprobs - delta)).astype(jnp.bfloat16)
        grad_q.append(
            (jnp.dot(dscores, key_head, preferred_element_type=jnp.float32) * score_scale).astype(
                jnp.bfloat16
            )
        )
        grad_k.append(
            (
                jnp.einsum("qk,qd->kd", dscores, query_head, preferred_element_type=jnp.float32)
                * score_scale
            ).astype(jnp.bfloat16)
        )
        grad_v.append(
            jnp.einsum(
                "qk,qd->kd", probs_low, grad_head, preferred_element_type=jnp.float32
            ).astype(jnp.bfloat16)
        )
    return (
        jnp.concatenate(grad_q, axis=1),
        jnp.concatenate(grad_k, axis=1),
        jnp.concatenate(grad_v, axis=1),
    )


def by_clusters(queries, key_rows, value_rows, out_weight, grad_output, cluster_ids, block_pattern):
    tokens = queries.shape[0]
    width = queries.shape[1]
    head_count = width // HD
    groups = lax.axis_size("seq")
    slot_rows = 2 * tokens // groups
    slot_total = groups * slot_rows
    blocks = block_pattern.shape[1]
    owner_index = lax.axis_index("seq")
    score_scale = 1.0 / math.sqrt(HD)
    members = (cluster_ids[:, None] == jnp.arange(groups, dtype=jnp.int32)[None, :]).astype(
        jnp.int32
    )
    earlier = jnp.cumsum(members, axis=0) - members
    local_rank = jnp.sum(earlier * members, axis=1)
    send_counts = jnp.sum(members, axis=0)
    slot_index = cluster_ids * slot_rows + local_rank

    def to_slots(row_data):
        return (
            jnp.zeros((slot_total, row_data.shape[1]), row_data.dtype).at[slot_index].set(row_data)
        )

    def from_slots(buffer):
        return jnp.take(buffer, slot_index, axis=0)

    full_weight = lax.all_gather(out_weight, "seq", axis=1, tiled=True)
    query_in, key_in, value_in, got_counts = (
        lax.all_to_all(to_slots(queries), "seq", split_axis=0, concat_axis=0, tiled=True),
        lax.all_to_all(to_slots(key_rows), "seq", split_axis=0, concat_axis=0, tiled=True),
        lax.all_to_all(to_slots(value_rows), "seq", split_axis=0, concat_axis=0, tiled=True),
        lax.all_to_all(send_counts, "seq", split_axis=0, concat_axis=0, tiled=True),
    )
    offsets = jnp.cumsum(got_counts) - got_counts
    pattern = lax.dynamic_index_in_dim(block_pattern, owner_index, 0, keepdims=False).astype(
        jnp.float32
    )
    slot_source = jnp.arange(slot_total, dtype=jnp.int32) // slot_rows
    slot_place = jnp.arange(slot_total, dtype=jnp.int32) % slot_rows
    row_live = slot_place < jnp.take(got_counts, slot_source)
    rank_rows = jnp.take(offsets, slot_source) + slot_place
    query_side, key_side, value_side = (query_in, key_in, value_in)
    onehot = (rank_rows[:, None] // BLK == jnp.arange(blocks, dtype=jnp.int32)[None, :]).astype(
        jnp.float32
    )
    block_ok = jnp.dot(jnp.dot(onehot, pattern), onehot.T) > 0.5
    usable = (
        block_ok
        & (rank_rows[None, :] <= rank_rows[:, None])
        & row_live[None, :]
        & row_live[:, None]
    )
    diagonal = jnp.eye(rank_rows.shape[0], dtype=bool)
    allowed = usable | diagonal & ~row_live[:, None]
    attn_side = attend(query_side, key_side, value_side, allowed, head_count, score_scale)
    attn_local = from_slots(
        lax.all_to_all(attn_side, "seq", split_axis=0, concat_axis=0, tiled=True)
    )
    partial_value = jnp.dot(attn_local, full_weight, preferred_element_type=jnp.float32)
    rounded_part = lax.optimization_barrier(partial_value.astype(jnp.bfloat16)).astype(jnp.float32)
    layer_out = lax.psum_scatter(
        rounded_part.astype(jnp.bfloat16), "head", scatter_dimension=1, tiled=True
    )
    grad_sum = jnp.einsum(
        "td,wd->tw",
        lax.all_gather(grad_output, "head", axis=1, tiled=True),
        full_weight,
        preferred_element_type=jnp.float32,
    )
    grad_attention = grad_sum.astype(jnp.bfloat16)
    grad_in = lax.all_to_all(
        to_slots(grad_attention), "seq", split_axis=0, concat_axis=0, tiled=True
    )
    grad_q, grad_k, grad_v = attend_back(
        query_side, key_side, value_side, allowed, attn_side, grad_in, head_count, score_scale
    )
    back_q, back_k, back_v = (
        lax.all_to_all(grad_q, "seq", split_axis=0, concat_axis=0, tiled=True),
        lax.all_to_all(grad_k, "seq", split_axis=0, concat_axis=0, tiled=True),
        lax.all_to_all(grad_v, "seq", split_axis=0, concat_axis=0, tiled=True),
    )
    return (layer_out, from_slots(back_q), from_slots(back_k), from_slots(back_v))


ID_ROWS = 16
MESH = pl.DeviceIdType.MESH


def one_hot(hit):
    return jnp.where(hit, 1.0, 0.0).astype(jnp.bfloat16)


def dot_rows(left, right):
    return lax.dot_general(
        left, right, (((1,), (0,)), ((), ())), preferred_element_type=jnp.float32
    )


def dot_last(left, right):
    return lax.dot_general(
        left, right, (((1,), (1,)), ((), ())), preferred_element_type=jnp.float32
    )


def dot_first(left, right):
    return lax.dot_general(
        left, right, (((0,), (0,)), ((), ())), preferred_element_type=jnp.float32
    )


def cluster_places(ids_ref, rows, parts, place_ref, place_cols_ref):
    before = lax.broadcasted_iota(jnp.int32, (rows, rows), 0)
    after = lax.broadcasted_iota(jnp.int32, (rows, rows), 1)
    strict = one_hot(before < after)
    names = lax.broadcasted_iota(jnp.int32, (parts, rows), 0).astype(jnp.float32)
    seen = jnp.zeros((parts, 1), jnp.float32)
    lines = []
    for part in range(parts):
        ids = jnp.concatenate(
            [
                ids_ref[part, i : i + 1, :].astype(jnp.float32)
                for i in range(rows // HD)
            ],
            axis=1,
        )
        hit = names == ids
        mark = jnp.where(hit, 1.0, 0.0)
        rank = dot_rows(mark.astype(jnp.bfloat16), strict) + seen
        lines.append(jnp.sum(mark * (rank + names * rows), axis=0, keepdims=True))
        seen = seen + jnp.sum(mark, axis=1, keepdims=True)
    places = jnp.concatenate(lines, axis=0)
    place_ref[...] = places
    padded = jnp.concatenate([places, jnp.zeros((HD - parts, rows), jnp.float32)], axis=0)
    place_cols_ref[...] = padded.T


def to_cluster(place_ref, rows, parts, cluster, read_part):
    want = lax.broadcasted_iota(jnp.int32, (rows, rows), 0).astype(jnp.float32) + (
        cluster * rows
    ).astype(jnp.float32)
    total = None
    for part in range(parts):
        pick = one_hot(want == place_ref[part : part + 1, :])
        term = dot_rows(pick, read_part(part))
        total = term if total is None else total + term
    return total.astype(jnp.bfloat16)


def from_clusters(place_cols_ref, rows, parts, part, ordered):
    lanes = lax.broadcasted_iota(jnp.int32, (rows, parts * rows), 1).astype(jnp.float32)
    pick = one_hot(place_cols_ref[:, part : part + 1] == lanes)
    return dot_rows(pick, ordered).astype(jnp.bfloat16)


def cluster_probs(pattern_ref, cluster, query, key, rows, score_scale):
    scores = dot_last(query, key) * score_scale
    row_at = lax.broadcasted_iota(jnp.int32, (rows, rows), 0)
    col_at = lax.broadcasted_iota(jnp.int32, (rows, rows), 1)
    reads = pattern_ref[cluster * 4 + 2]
    ok = (col_at <= row_at) & ((row_at // BLK == col_at // BLK) | (reads == 1))
    scores = jnp.where(ok, scores, -jnp.inf)
    shifted = jnp.exp(scores - jnp.max(scores, axis=1, keepdims=True))
    return shifted / jnp.sum(shifted, axis=1, keepdims=True)


def layer_kernel(
    rows, parts, groups, pattern_ref, ids_ref, q_ref, k_ref, v_ref, w_ref, g_ref,
    out_ref, gq_ref, gk_ref, gv_ref,
    q_in, k_in, v_in, ids_in, weight, cotangent, places, place_cols, ordered, probs_at, held,
    mixed_send, attn, grad_sum, grad_send, grad_in, dscores_at, held_qk, held_v, back_q, back_k, back_v,
    partial, shares,
    tok_send, tok_recv, ring_send, ring_recv, head_send, head_recv, own_sem,
):
    score_scale = 1.0 / math.sqrt(HD)
    me = lax.axis_index("seq")
    group = lax.axis_index("head")
    half = w_ref.shape[0] // 2
    cols = w_ref.shape[1]

    def other(j):
        return lax.rem(me + j, parts)

    def other_group(j):
        return lax.rem(group + j, groups)

    def head_at(index):
        return pl.ds(pl.multiple_of(index * HD, HD), HD)

    def along_seq(kind, j, source, target):
        return pltpu.make_async_remote_copy(
            src_ref=source, dst_ref=target, send_sem=tok_send.at[kind, j],
            recv_sem=tok_recv.at[kind, j], device_id={"seq": other(j)}, device_id_type=MESH,
        )

    def along_head(kind, j, source, target):
        return pltpu.make_async_remote_copy(
            src_ref=source, dst_ref=target, send_sem=head_send.at[kind, j],
            recv_sem=head_recv.at[kind, j], device_id={"head": other_group(j)}, device_id_type=MESH,
        )

    line = parts // 2
    row, side = me // 2, lax.rem(me, 2)
    place = row + side * (parts - 1 - 2 * row)

    def at_place(p):
        p = lax.rem(p + 2 * parts, parts)
        far = p // line
        return 2 * (p + far * (parts - 1 - 2 * p)) + far

    def ring(way, step):
        sign = 1 - 2 * way
        block = weight.at[at_place(place - sign * step), pl.ds(way * half, half)]
        return pltpu.make_async_remote_copy(
            src_ref=block, dst_ref=block, send_sem=ring_send.at[way, step],
            recv_sem=ring_recv.at[way, step], device_id={"seq": at_place(place + sign)},
            device_id_type=MESH,
        )

    own_weight = pltpu.make_async_copy(w_ref, weight.at[me], own_sem.at[0])
    own_weight.start()
    for i in range(2):
        cotangent[2 * group + i] = g_ref[:, i * cols : (i + 1) * cols]

    barrier = pltpu.get_barrier_semaphore()
    for j in range(1, parts):
        pl.semaphore_signal(barrier, inc=1, device_id={"seq": other(j)}, device_id_type=MESH)
    for j in range(1, groups):
        pl.semaphore_signal(barrier, inc=1, device_id={"head": other_group(j)}, device_id_type=MESH)
    pl.semaphore_wait(barrier, parts + groups - 2)

    own_weight.wait()
    for way in range(2):
        ring(way, 0).start()

    def head_copies(j):
        block = cotangent.at[pl.ds(2 * group, 2)]
        return along_head(0, j, block, block)

    for j in range(1, groups):
        head_copies(j).start()

    def token_copies(j):
        dest = head_at(other(j))
        return (
            along_seq(0, j, q_ref.at[:, dest], q_in.at[me]),
            along_seq(1, j, k_ref.at[:, dest], k_in.at[me]),
            along_seq(2, j, v_ref.at[:, dest], v_in.at[me]),
            along_seq(3, j, ids_ref, ids_in.at[me]),
        )

    for j in range(1, parts):
        for copy in token_copies(j):
            copy.start()
    q_in[me] = q_ref[:, head_at(me)]
    k_in[me] = k_ref[:, head_at(me)]
    v_in[me] = v_ref[:, head_at(me)]
    ids_in[me] = ids_ref[...]

    grad_sum[...] = jnp.zeros_like(grad_sum)

    for j in range(1, groups):
        head_copies(j).wait()

    def accumulate(way, owner):
        lanes = slice(way * half, (way + 1) * half)
        grad_sum[:, lanes] += dot_last(cotangent[owner], weight[owner, lanes, :])

    for way in range(2):
        accumulate(way, me)

    def pump(step, last):
        for way in range(2):
            ring(way, step).wait()
            if not last:
                ring(way, step + 1).start()
        for way in range(2):
            accumulate(way, at_place(place - (1 - 2 * way) * (step + 1)))

    def early(step, _):
        pump(step, False)
        return 0

    lax.fori_loop(0, 2, early, 0)
    for j in range(1, parts):
        for copy in token_copies(j):
            copy.wait()
    cluster_places(ids_in, rows, parts, places, place_cols)

    def read_part(part):
        return jnp.concatenate([q_in[part], k_in[part], v_in[part]], axis=1)

    def attend_cluster(cluster):
        picked = to_cluster(places, rows, parts, cluster, read_part)
        ordered[cluster] = picked
        query, key, value = (picked[:, i * HD : (i + 1) * HD] for i in range(3))
        probs = cluster_probs(pattern_ref, cluster, query, key, rows, score_scale)
        probs_at[cluster] = probs
        at = pl.multiple_of(cluster * rows, rows)
        held[pl.ds(at, rows), :] = dot_rows(probs.astype(jnp.bfloat16), value).astype(jnp.bfloat16)

    def middle(step, _):
        pump(step, False)
        attend_cluster(2 * (step - 2))
        attend_cluster(2 * (step - 2) + 1)
        return 0

    lax.fori_loop(2, 2 + line, middle, 0)
    for part in range(parts):
        mixed_send[part] = from_clusters(place_cols, rows, parts, part, held[...])

    def attn_copy(j):
        return along_seq(4, j, mixed_send.at[other(j)], attn.at[:, head_at(me)])

    for j in range(1, parts):
        attn_copy(j).start()
    attn[:, head_at(me)] = mixed_send[me]

    pump(parts - 2, True)
    for part in range(parts):
        grad_send[part] = grad_sum[:, part * HD : (part + 1) * HD].astype(jnp.bfloat16)

    def grad_copy(j):
        return along_seq(5, j, grad_send.at[other(j)], grad_in.at[me])

    for j in range(1, parts):
        grad_copy(j).start()
    grad_in[me] = grad_send[me]

    for j in range(1, parts):
        attn_copy(j).wait()

    def project(owner, _):
        partial[owner] = dot_rows(attn[...], weight[owner]).astype(jnp.bfloat16)
        return 0

    lax.fori_loop(0, parts, project, 0)

    def share_copy(j):
        return along_head(1, j, partial.at[pl.ds(2 * other_group(j), 2)], shares.at[group])

    for j in range(1, groups):
        share_copy(j).start()
    shares[group] = partial[pl.ds(2 * group, 2)]

    for j in range(1, parts):
        grad_copy(j).wait()

    def back_values(cluster, _):
        grad = to_cluster(places, rows, parts, cluster, lambda part: grad_in[part])
        value = ordered[cluster, :, 2 * HD : 3 * HD]
        probs = probs_at[cluster]
        here = pl.ds(pl.multiple_of(cluster * rows, rows), rows)
        delta = jnp.sum(
            grad.astype(jnp.float32) * held[here, :].astype(jnp.float32), axis=1, keepdims=True
        )
        dscores_at[cluster] = (probs * (dot_last(grad, value) - delta)).astype(jnp.bfloat16)
        held_v[here, :] = dot_first(probs.astype(jnp.bfloat16), grad).astype(jnp.bfloat16)
        return 0

    lax.fori_loop(0, parts, back_values, 0, unroll=2)
    for part in range(parts):
        back_v[part] = from_clusters(place_cols, rows, parts, part, held_v[...])

    def value_copy(j):
        return along_seq(6, j, back_v.at[other(j)], gv_ref.at[:, head_at(me)])

    for j in range(1, parts):
        value_copy(j).start()
    gv_ref[:, head_at(me)] = back_v[me]

    def back_scores(cluster, _):
        query, key = (ordered[cluster, :, i * HD : (i + 1) * HD] for i in range(2))
        dscores = dscores_at[cluster]
        here = pl.ds(pl.multiple_of(cluster * rows, rows), rows)
        held_qk[here, 0:HD] = (dot_rows(dscores, key) * score_scale).astype(jnp.bfloat16)
        held_qk[here, HD:] = (dot_first(dscores, query) * score_scale).astype(jnp.bfloat16)
        return 0

    lax.fori_loop(0, parts, back_scores, 0, unroll=2)
    for part in range(parts):
        back = from_clusters(place_cols, rows, parts, part, held_qk[...])
        back_q[part] = back[:, :HD]
        back_k[part] = back[:, HD:]

    def pair_copies(j):
        return (
            along_seq(7, j, back_q.at[other(j)], gq_ref.at[:, head_at(me)]),
            along_seq(8, j, back_k.at[other(j)], gk_ref.at[:, head_at(me)]),
        )

    for j in range(1, parts):
        for copy in pair_copies(j):
            copy.start()
    gq_ref[:, head_at(me)] = back_q[me]
    gk_ref[:, head_at(me)] = back_k[me]

    for j in range(1, groups):
        share_copy(j).wait()
    for i in range(2):
        total = shares[0, i].astype(jnp.float32)
        for j in range(1, groups):
            total = total + shares[j, i].astype(jnp.float32)
        out_ref[:, i * cols : (i + 1) * cols] = total.astype(jnp.bfloat16)

    for j in range(1, parts):
        value_copy(j).wait()
        for copy in pair_copies(j):
            copy.wait()


VMEM_SPEC = pl.BlockSpec(memory_space=pltpu.VMEM)
SMEM_SPEC = pl.BlockSpec(memory_space=pltpu.SMEM)


def by_heads(queries, key_rows, value_rows, out_weight, grad_output, cluster_ids, block_pattern):
    rows, width = queries.shape
    parts = lax.axis_size("seq")
    groups = lax.axis_size("head")
    depth, cols = out_weight.shape
    id_rows = jnp.pad(
        cluster_ids.reshape(-1, HD).astype(jnp.bfloat16), ((0, ID_ROWS - rows // HD), (0, 0))
    )
    low, full = jnp.bfloat16, jnp.float32

    def vmem(*shape, kind=low):
        return pltpu.VMEM(shape, kind)

    scratch = [
        vmem(parts, rows, HD), vmem(parts, rows, HD), vmem(parts, rows, HD),
        vmem(parts, ID_ROWS, HD), vmem(parts, depth, cols), vmem(parts, rows, cols),
        vmem(parts, rows, kind=full), vmem(rows, HD, kind=full), vmem(parts, rows, 3 * HD),
        vmem(parts, rows, rows, kind=full), vmem(parts * rows, HD), vmem(parts, rows, HD),
        vmem(rows, width), vmem(rows, width, kind=full), vmem(parts, rows, HD),
        vmem(parts, rows, HD), vmem(parts, rows, rows), vmem(parts * rows, 2 * HD),
        vmem(parts * rows, HD), vmem(parts, rows, HD), vmem(parts, rows, HD), vmem(parts, rows, HD),
        vmem(parts, rows, cols), vmem(groups, 2, rows, cols),
        pltpu.SemaphoreType.DMA((9, parts)), pltpu.SemaphoreType.DMA((9, parts)),
        pltpu.SemaphoreType.DMA((2, parts)), pltpu.SemaphoreType.DMA((2, parts)),
        pltpu.SemaphoreType.DMA((2, groups)), pltpu.SemaphoreType.DMA((2, groups)),
        pltpu.SemaphoreType.DMA((1,)),
    ]
    return pl.pallas_call(
        functools.partial(layer_kernel, rows, parts, groups),
        out_shape=(jax.ShapeDtypeStruct((rows, width), low),) * 4,
        in_specs=[SMEM_SPEC] + [VMEM_SPEC] * 6,
        out_specs=(VMEM_SPEC,) * 4,
        scratch_shapes=scratch,
        compiler_params=pltpu.CompilerParams(
            collective_id=0, has_side_effects=True, vmem_limit_bytes=56 * 1024 * 1024
        ),
        name="routing_layer",
    )(block_pattern.reshape(-1), id_rows, queries, key_rows, value_rows, out_weight, grad_output)


def on_device(queries, *others):
    heads = queries.shape[1] // HD
    parts, groups = lax.axis_size("seq"), lax.axis_size("head")
    if heads == parts == 2 * groups and others[-1].shape[1] == 2:
        return by_heads(queries, *others)
    return by_clusters(queries, *others)


def solution(mesh):
    in_specs = (
        P("seq", "head"),
        P("seq", "head"),
        P("seq", "head"),
        P("head", "seq"),
        P("seq", "head"),
        P("seq"),
        P(),
    )
    out_specs = (P("seq", "head"), P("seq", "head"), P("seq", "head"), P("seq", "head"))
    return jax.shard_map(
        on_device, mesh=mesh, in_specs=in_specs, out_specs=out_specs, check_vma=False
    )
```

```python
import functools
import math

import jax
import jax.numpy as jnp
from jax import lax
from jax.experimental import pallas as pl
from jax.experimental.pallas import tpu as pltpu
from jax.sharding import PartitionSpec as P

HD = 128
BLK = 128


def probabilities(query_part, key_part, allowed, score_scale):
    scores = (
        jnp.einsum("qd,kd->qk", query_part, key_part, preferred_element_type=jnp.float32)
        * score_scale
    )
    scores = jnp.where(allowed, scores, -jnp.inf)
    shifted = jnp.exp(scores - jnp.max(scores, axis=1, keepdims=True))
    return shifted / jnp.sum(shifted, axis=1, keepdims=True)


def attend(query_side, key_side, value_side, allowed, head_count, score_scale):
    results = []
    for which_head in range(head_count):
        lower = which_head * HD
        probs = probabilities(
            query_side[:, lower : lower + HD], key_side[:, lower : lower + HD], allowed, score_scale
        )
        mixed = jnp.dot(
            probs.astype(jnp.bfloat16),
            value_side[:, lower : lower + HD],
            preferred_element_type=jnp.float32,
        )
        results.append(mixed.astype(jnp.bfloat16))
    return jnp.concatenate(results, axis=1)


def attend_back(
    query_side, key_side, value_side, allowed, attn_side, grad_side, head_count, score_scale
):
    grad_q, grad_k, grad_v = ([], [], [])
    for which_head in range(head_count):
        lower = which_head * HD
        query_head = query_side[:, lower : lower + HD]
        key_head = key_side[:, lower : lower + HD]
        value_head = value_side[:, lower : lower + HD]
        grad_head = grad_side[:, lower : lower + HD]
        attn_head = attn_side[:, lower : lower + HD]
        probs = probabilities(query_head, key_head, allowed, score_scale)
        probs_low = probs.astype(jnp.bfloat16)
        delta = jnp.sum(
            grad_head.astype(jnp.float32) * attn_head.astype(jnp.float32), axis=1, keepdims=True
        )
        dprobs = jnp.einsum("qd,kd->qk", grad_head, value_head, preferred_element_type=jnp.float32)
        dscores = (probs * (dprobs - delta)).astype(jnp.bfloat16)
        grad_q.append(
            (jnp.dot(dscores, key_head, preferred_element_type=jnp.float32) * score_scale).astype(
                jnp.bfloat16
            )
        )
        grad_k.append(
            (
                jnp.einsum("qk,qd->kd", dscores, query_head, preferred_element_type=jnp.float32)
                * score_scale
            ).astype(jnp.bfloat16)
        )
        grad_v.append(
            jnp.einsum(
                "qk,qd->kd", probs_low, grad_head, preferred_element_type=jnp.float32
            ).astype(jnp.bfloat16)
        )
    return (
        jnp.concatenate(grad_q, axis=1),
        jnp.concatenate(grad_k, axis=1),
        jnp.concatenate(grad_v, axis=1),
    )


def by_clusters(queries, key_rows, value_rows, out_weight, grad_output, cluster_ids, block_pattern):
    tokens = queries.shape[0]
    width = queries.shape[1]
    head_count = width // HD
    groups = lax.axis_size("seq")
    slot_rows = 2 * tokens // groups
    slot_total = groups * slot_rows
    blocks = block_pattern.shape[1]
    owner_index = lax.axis_index("seq")
    score_scale = 1.0 / math.sqrt(HD)
    members = (cluster_ids[:, None] == jnp.arange(groups, dtype=jnp.int32)[None, :]).astype(
        jnp.int32
    )
    earlier = jnp.cumsum(members, axis=0) - members
    local_rank = jnp.sum(earlier * members, axis=1)
    send_counts = jnp.sum(members, axis=0)
    slot_index = cluster_ids * slot_rows + local_rank

    def to_slots(row_data):
        return (
            jnp.zeros((slot_total, row_data.shape[1]), row_data.dtype).at[slot_index].set(row_data)
        )

    def from_slots(buffer):
        return jnp.take(buffer, slot_index, axis=0)

    full_weight = lax.all_gather(out_weight, "seq", axis=1, tiled=True)
    query_in, key_in, value_in, got_counts = (
        lax.all_to_all(to_slots(queries), "seq", split_axis=0, concat_axis=0, tiled=True),
        lax.all_to_all(to_slots(key_rows), "seq", split_axis=0, concat_axis=0, tiled=True),
        lax.all_to_all(to_slots(value_rows), "seq", split_axis=0, concat_axis=0, tiled=True),
        lax.all_to_all(send_counts, "seq", split_axis=0, concat_axis=0, tiled=True),
    )
    offsets = jnp.cumsum(got_counts) - got_counts
    pattern = lax.dynamic_index_in_dim(block_pattern, owner_index, 0, keepdims=False).astype(
        jnp.float32
    )
    slot_source = jnp.arange(slot_total, dtype=jnp.int32) // slot_rows
    slot_place = jnp.arange(slot_total, dtype=jnp.int32) % slot_rows
    row_live = slot_place < jnp.take(got_counts, slot_source)
    rank_rows = jnp.take(offsets, slot_source) + slot_place
    query_side, key_side, value_side = (query_in, key_in, value_in)
    onehot = (rank_rows[:, None] // BLK == jnp.arange(blocks, dtype=jnp.int32)[None, :]).astype(
        jnp.float32
    )
    block_ok = jnp.dot(jnp.dot(onehot, pattern), onehot.T) > 0.5
    usable = (
        block_ok
        & (rank_rows[None, :] <= rank_rows[:, None])
        & row_live[None, :]
        & row_live[:, None]
    )
    diagonal = jnp.eye(rank_rows.shape[0], dtype=bool)
    allowed = usable | diagonal & ~row_live[:, None]
    attn_side = attend(query_side, key_side, value_side, allowed, head_count, score_scale)
    attn_local = from_slots(
        lax.all_to_all(attn_side, "seq", split_axis=0, concat_axis=0, tiled=True)
    )
    partial_value = jnp.dot(attn_local, full_weight, preferred_element_type=jnp.float32)
    rounded_part = lax.optimization_barrier(partial_value.astype(jnp.bfloat16)).astype(jnp.float32)
    layer_out = lax.psum_scatter(
        rounded_part.astype(jnp.bfloat16), "head", scatter_dimension=1, tiled=True
    )
    grad_sum = jnp.einsum(
        "td,wd->tw",
        lax.all_gather(grad_output, "head", axis=1, tiled=True),
        full_weight,
        preferred_element_type=jnp.float32,
    )
    grad_attention = grad_sum.astype(jnp.bfloat16)
    grad_in = lax.all_to_all(
        to_slots(grad_attention), "seq", split_axis=0, concat_axis=0, tiled=True
    )
    grad_q, grad_k, grad_v = attend_back(
        query_side, key_side, value_side, allowed, attn_side, grad_in, head_count, score_scale
    )
    back_q, back_k, back_v = (
        lax.all_to_all(grad_q, "seq", split_axis=0, concat_axis=0, tiled=True),
        lax.all_to_all(grad_k, "seq", split_axis=0, concat_axis=0, tiled=True),
        lax.all_to_all(grad_v, "seq", split_axis=0, concat_axis=0, tiled=True),
    )
    return (layer_out, from_slots(back_q), from_slots(back_k), from_slots(back_v))


ID_ROWS = 16
EARLY = 6
MESH = pl.DeviceIdType.MESH


def one_hot(hit):
    return jnp.where(hit, 1.0, 0.0).astype(jnp.bfloat16)


def dot_rows(left, right):
    return lax.dot_general(
        left, right, (((1,), (0,)), ((), ())), preferred_element_type=jnp.float32
    )


def dot_last(left, right):
    return lax.dot_general(
        left, right, (((1,), (1,)), ((), ())), preferred_element_type=jnp.float32
    )


def dot_first(left, right):
    return lax.dot_general(
        left, right, (((0,), (0,)), ((), ())), preferred_element_type=jnp.float32
    )


def cluster_places(ids_ref, rows, parts, place_ref, place_cols_ref):
    before = lax.broadcasted_iota(jnp.int32, (rows, rows), 0)
    after = lax.broadcasted_iota(jnp.int32, (rows, rows), 1)
    strict = one_hot(before < after)
    names = lax.broadcasted_iota(jnp.int32, (parts, rows), 0).astype(jnp.float32)
    seen = jnp.zeros((parts, 1), jnp.float32)
    lines = []
    for part in range(parts):
        ids = jnp.concatenate(
            [
                ids_ref[part, i : i + 1, :].astype(jnp.float32)
                for i in range(rows // HD)
            ],
            axis=1,
        )
        hit = names == ids
        mark = jnp.where(hit, 1.0, 0.0)
        rank = dot_rows(mark.astype(jnp.bfloat16), strict) + seen
        lines.append(jnp.sum(mark * (rank + names * rows), axis=0, keepdims=True))
        seen = seen + jnp.sum(mark, axis=1, keepdims=True)
    places = jnp.concatenate(lines, axis=0)
    place_ref[...] = places
    padded = jnp.concatenate([places, jnp.zeros((HD - parts, rows), jnp.float32)], axis=0)
    place_cols_ref[...] = padded.T


def to_cluster(place_ref, rows, parts, cluster, read_part):
    want = lax.broadcasted_iota(jnp.int32, (rows, rows), 0).astype(jnp.float32) + (
        cluster * rows
    ).astype(jnp.float32)
    total = None
    for part in range(parts):
        pick = one_hot(want == place_ref[part : part + 1, :])
        term = dot_rows(pick, read_part(part))
        total = term if total is None else total + term
    return total.astype(jnp.bfloat16)


def from_clusters(place_cols_ref, rows, parts, part, ordered):
    lanes = lax.broadcasted_iota(jnp.int32, (rows, parts * rows), 1).astype(jnp.float32)
    pick = one_hot(place_cols_ref[:, part : part + 1] == lanes)
    return dot_rows(pick, ordered).astype(jnp.bfloat16)


def cluster_probs(pattern_ref, cluster, query, key, rows, score_scale):
    scores = dot_last(query, key) * score_scale
    row_at = lax.broadcasted_iota(jnp.int32, (rows, rows), 0)
    col_at = lax.broadcasted_iota(jnp.int32, (rows, rows), 1)
    reads = pattern_ref[cluster * 4 + 2]
    ok = (col_at <= row_at) & ((row_at // BLK == col_at // BLK) | (reads == 1))
    scores = jnp.where(ok, scores, -jnp.inf)
    shifted = jnp.exp(scores - jnp.max(scores, axis=1, keepdims=True))
    return shifted / jnp.sum(shifted, axis=1, keepdims=True)


def layer_kernel(
    rows, parts, groups, pattern_ref, ids_ref, q_ref, k_ref, v_ref, w_ref, g_ref,
    out_ref, gq_ref, gk_ref, gv_ref,
    q_in, k_in, v_in, ids_in, weight, cotangent, places, place_cols, ordered, probs_at, held,
    mixed_send, attn, grad_sum, grad_send, grad_in, dscores_at, held_qk, held_v, back_q, back_k, back_v,
    partial, shares,
    tok_send, tok_recv, ring_send, ring_recv, head_send, head_recv, own_sem,
):
    score_scale = 1.0 / math.sqrt(HD)
    me = lax.axis_index("seq")
    group = lax.axis_index("head")
    half = w_ref.shape[0] // 2
    quarter = half // 2
    ticks = 2 * (parts - 1)
    cols = w_ref.shape[1]

    def other(j):
        return lax.rem(me + j, parts)

    def other_group(j):
        return lax.rem(group + j, groups)

    def head_at(index):
        return pl.ds(pl.multiple_of(index * HD, HD), HD)

    def along_seq(kind, j, source, target):
        return pltpu.make_async_remote_copy(
            src_ref=source, dst_ref=target, send_sem=tok_send.at[kind, j],
            recv_sem=tok_recv.at[kind, j], device_id={"seq": other(j)}, device_id_type=MESH,
        )

    def along_head(kind, j, source, target):
        return pltpu.make_async_remote_copy(
            src_ref=source, dst_ref=target, send_sem=head_send.at[kind, j],
            recv_sem=head_recv.at[kind, j], device_id={"head": other_group(j)}, device_id_type=MESH,
        )

    line = parts // 2
    row, side = me // 2, lax.rem(me, 2)
    place = row + side * (parts - 1 - 2 * row)

    def at_place(p):
        p = lax.rem(p + 2 * parts, parts)
        far = p // line
        return 2 * (p + far * (parts - 1 - 2 * p)) + far

    def ring(way, tick):
        sign = 1 - 2 * way
        at = pl.multiple_of(way * half + lax.rem(tick, 2) * quarter, quarter)
        block = weight.at[at_place(place - sign * (tick // 2)), pl.ds(at, quarter)]
        return pltpu.make_async_remote_copy(
            src_ref=block, dst_ref=block, send_sem=ring_send.at[way, tick],
            recv_sem=ring_recv.at[way, tick], device_id={"seq": at_place(place + sign)},
            device_id_type=MESH,
        )

    own_weight = pltpu.make_async_copy(w_ref, weight.at[me], own_sem.at[0])
    own_weight.start()
    for i in range(2):
        cotangent[2 * group + i] = g_ref[:, i * cols : (i + 1) * cols]

    barrier = pltpu.get_barrier_semaphore()
    for j in range(1, parts):
        pl.semaphore_signal(barrier, inc=1, device_id={"seq": other(j)}, device_id_type=MESH)
    for j in range(1, groups):
        pl.semaphore_signal(barrier, inc=1, device_id={"head": other_group(j)}, device_id_type=MESH)
    pl.semaphore_wait(barrier, parts + groups - 2)

    own_weight.wait()
    for tick in range(2):
        for way in range(2):
            ring(way, jnp.int32(tick)).start()

    def head_copies(j):
        block = cotangent.at[pl.ds(2 * group, 2)]
        return along_head(0, j, block, block)

    for j in range(1, groups):
        head_copies(j).start()

    def token_copies(j):
        dest = head_at(other(j))
        return (
            along_seq(0, j, q_ref.at[:, dest], q_in.at[me]),
            along_seq(1, j, k_ref.at[:, dest], k_in.at[me]),
            along_seq(2, j, v_ref.at[:, dest], v_in.at[me]),
            along_seq(3, j, ids_ref, ids_in.at[me]),
        )

    for j in range(1, parts):
        for copy in token_copies(j):
            copy.start()
    q_in[me] = q_ref[:, head_at(me)]
    k_in[me] = k_ref[:, head_at(me)]
    v_in[me] = v_ref[:, head_at(me)]
    ids_in[me] = ids_ref[...]

    def forward(tick):
        for way in range(2):
            ring(way, tick).wait_recv()

            @pl.when(tick + 2 < ticks)
            def _():
                ring(way, tick + 2).start()

    def accumulate(tick):
        for way in range(2):
            owner = at_place(place - (1 - 2 * way) * (tick // 2 + 1))
            at = pl.multiple_of(way * half + lax.rem(tick, 2) * quarter, quarter)
            here = pl.ds(at, quarter)
            grad_sum[:, here] += dot_last(cotangent[owner], weight[owner, here, :])

    def pass_on(tick, _):
        forward(tick)
        return 0

    def add_up(tick, _):
        accumulate(tick)
        return 0

    def pump(tick, _):
        forward(tick)
        accumulate(tick)
        return 0

    lax.fori_loop(0, 2, pass_on, 0)
    for j in range(1, groups):
        head_copies(j).wait()
    for i in range(4):
        lanes = slice(i * quarter, (i + 1) * quarter)
        grad_sum[:, lanes] = dot_last(cotangent[me], weight[me, lanes, :])
    lax.fori_loop(0, 2, add_up, 0)
    lax.fori_loop(2, EARLY, pump, 0)
    for j in range(1, parts):
        for copy in token_copies(j):
            copy.wait()
    cluster_places(ids_in, rows, parts, places, place_cols)

    def read_part(part):
        return jnp.concatenate([q_in[part], k_in[part], v_in[part]], axis=1)

    def attend_cluster(cluster):
        picked = to_cluster(places, rows, parts, cluster, read_part)
        ordered[cluster] = picked
        query, key, value = (picked[:, i * HD : (i + 1) * HD] for i in range(3))
        probs = cluster_probs(pattern_ref, cluster, query, key, rows, score_scale)
        probs_at[cluster] = probs
        at = pl.multiple_of(cluster * rows, rows)
        held[pl.ds(at, rows), :] = dot_rows(probs.astype(jnp.bfloat16), value).astype(jnp.bfloat16)

    def middle(tick, _):
        pump(tick, 0)
        attend_cluster(tick - EARLY)
        return 0

    lax.fori_loop(EARLY, EARLY + parts - 1, middle, 0)
    attend_cluster(jnp.int32(parts - 1))
    lax.fori_loop(EARLY + parts - 1, ticks, pump, 0)
    def attn_copy(j):
        return along_seq(4, j, mixed_send.at[other(j)], attn.at[:, head_at(me)])

    for part in range(parts):
        grad_send[part] = grad_sum[:, part * HD : (part + 1) * HD].astype(jnp.bfloat16)

    def grad_copy(j):
        return along_seq(5, j, grad_send.at[other(j)], grad_in.at[me])

    for j in range(1, parts):
        grad_copy(j).start()
    grad_in[me] = grad_send[me]

    for part in range(parts):
        mixed_send[part] = from_clusters(place_cols, rows, parts, part, held[...])
    for j in range(1, parts):
        attn_copy(j).start()
    attn[:, head_at(me)] = mixed_send[me]

    for j in range(1, parts):
        grad_copy(j).wait()

    def back_values(cluster, _):
        grad = to_cluster(places, rows, parts, cluster, lambda part: grad_in[part])
        value = ordered[cluster, :, 2 * HD : 3 * HD]
        probs = probs_at[cluster]
        here = pl.ds(pl.multiple_of(cluster * rows, rows), rows)
        delta = jnp.sum(
            grad.astype(jnp.float32) * held[here, :].astype(jnp.float32), axis=1, keepdims=True
        )
        dscores_at[cluster] = (probs * (dot_last(grad, value) - delta)).astype(jnp.bfloat16)
        held_v[here, :] = dot_first(probs.astype(jnp.bfloat16), grad).astype(jnp.bfloat16)
        return 0

    lax.fori_loop(0, parts, back_values, 0, unroll=2)
    for part in range(parts):
        back_v[part] = from_clusters(place_cols, rows, parts, part, held_v[...])

    def value_copy(j):
        return along_seq(6, j, back_v.at[other(j)], gv_ref.at[:, head_at(me)])

    for j in range(1, parts):
        value_copy(j).start()
    gv_ref[:, head_at(me)] = back_v[me]

    def back_scores(cluster, _):
        query, key = (ordered[cluster, :, i * HD : (i + 1) * HD] for i in range(2))
        dscores = dscores_at[cluster]
        here = pl.ds(pl.multiple_of(cluster * rows, rows), rows)
        held_qk[here, 0:HD] = (dot_rows(dscores, key) * score_scale).astype(jnp.bfloat16)
        held_qk[here, HD:] = (dot_first(dscores, query) * score_scale).astype(jnp.bfloat16)
        return 0

    lax.fori_loop(0, parts, back_scores, 0, unroll=2)
    for part in range(parts):
        back = from_clusters(place_cols, rows, parts, part, held_qk[...])
        back_q[part] = back[:, :HD]
        back_k[part] = back[:, HD:]

    def pair_copies(j):
        return (
            along_seq(7, j, back_q.at[other(j)], gq_ref.at[:, head_at(me)]),
            along_seq(8, j, back_k.at[other(j)], gk_ref.at[:, head_at(me)]),
        )

    for j in range(1, parts):
        for copy in pair_copies(j):
            copy.start()
    gq_ref[:, head_at(me)] = back_q[me]
    gk_ref[:, head_at(me)] = back_k[me]

    for j in range(1, parts):
        attn_copy(j).wait()

    def project(owner, _):
        partial[owner] = dot_rows(attn[...], weight[owner]).astype(jnp.bfloat16)
        return 0

    lax.fori_loop(0, parts, project, 0)

    def share_copy(j):
        return along_head(1, j, partial.at[pl.ds(2 * other_group(j), 2)], shares.at[group])

    for j in range(1, groups):
        share_copy(j).start()
    shares[group] = partial[pl.ds(2 * group, 2)]

    for j in range(1, groups):
        share_copy(j).wait()
    for i in range(2):
        total = shares[0, i].astype(jnp.float32)
        for j in range(1, groups):
            total = total + shares[j, i].astype(jnp.float32)
        out_ref[:, i * cols : (i + 1) * cols] = total.astype(jnp.bfloat16)

    for j in range(1, parts):
        value_copy(j).wait()
        for copy in pair_copies(j):
            copy.wait()

    def sent(tick, _):
        for way in range(2):
            ring(way, tick).wait_send()
        return 0

    lax.fori_loop(0, ticks, sent, 0)


VMEM_SPEC = pl.BlockSpec(memory_space=pltpu.VMEM)
SMEM_SPEC = pl.BlockSpec(memory_space=pltpu.SMEM)


def by_heads(queries, key_rows, value_rows, out_weight, grad_output, cluster_ids, block_pattern):
    rows, width = queries.shape
    parts = lax.axis_size("seq")
    groups = lax.axis_size("head")
    depth, cols = out_weight.shape
    id_rows = jnp.pad(
        cluster_ids.reshape(-1, HD).astype(jnp.bfloat16), ((0, ID_ROWS - rows // HD), (0, 0))
    )
    low, full = jnp.bfloat16, jnp.float32

    def vmem(*shape, kind=low):
        return pltpu.VMEM(shape, kind)

    scratch = [
        vmem(parts, rows, HD), vmem(parts, rows, HD), vmem(parts, rows, HD),
        vmem(parts, ID_ROWS, HD), vmem(parts, depth, cols), vmem(parts, rows, cols),
        vmem(parts, rows, kind=full), vmem(rows, HD, kind=full), vmem(parts, rows, 3 * HD),
        vmem(parts, rows, rows, kind=full), vmem(parts * rows, HD), vmem(parts, rows, HD),
        vmem(rows, width), vmem(rows, width, kind=full), vmem(parts, rows, HD),
        vmem(parts, rows, HD), vmem(parts, rows, rows), vmem(parts * rows, 2 * HD),
        vmem(parts * rows, HD), vmem(parts, rows, HD), vmem(parts, rows, HD), vmem(parts, rows, HD),
        vmem(parts, rows, cols), vmem(groups, 2, rows, cols),
        pltpu.SemaphoreType.DMA((9, parts)), pltpu.SemaphoreType.DMA((9, parts)),
        pltpu.SemaphoreType.DMA((2, 2 * parts)), pltpu.SemaphoreType.DMA((2, 2 * parts)),
        pltpu.SemaphoreType.DMA((2, groups)), pltpu.SemaphoreType.DMA((2, groups)),
        pltpu.SemaphoreType.DMA((1,)),
    ]
    return pl.pallas_call(
        functools.partial(layer_kernel, rows, parts, groups),
        out_shape=(jax.ShapeDtypeStruct((rows, width), low),) * 4,
        in_specs=[SMEM_SPEC] + [VMEM_SPEC] * 6,
        out_specs=(VMEM_SPEC,) * 4,
        scratch_shapes=scratch,
        compiler_params=pltpu.CompilerParams(
            collective_id=0, has_side_effects=True, vmem_limit_bytes=56 * 1024 * 1024
        ),
        name="routing_layer",
    )(block_pattern.reshape(-1), id_rows, queries, key_rows, value_rows, out_weight, grad_output)


def on_device(queries, *others):
    heads = queries.shape[1] // HD
    parts, groups = lax.axis_size("seq"), lax.axis_size("head")
    if heads == parts == 2 * groups and others[-1].shape[1] == 2:
        return by_heads(queries, *others)
    return by_clusters(queries, *others)


def solution(mesh):
    in_specs = (
        P("seq", "head"),
        P("seq", "head"),
        P("seq", "head"),
        P("head", "seq"),
        P("seq", "head"),
        P("seq"),
        P(),
    )
    out_specs = (P("seq", "head"), P("seq", "head"), P("seq", "head"), P("seq", "head"))
    return jax.shard_map(
        on_device, mesh=mesh, in_specs=in_specs, out_specs=out_specs, check_vma=False
    )
```

```python
import functools
import math

import jax
import jax.numpy as jnp
from jax import lax
from jax.experimental import pallas as pl
from jax.experimental.pallas import tpu as pltpu
from jax.sharding import PartitionSpec as P

HD = 128
BLK = 128


def probabilities(query_part, key_part, allowed, score_scale):
    scores = (
        jnp.einsum("qd,kd->qk", query_part, key_part, preferred_element_type=jnp.float32)
        * score_scale
    )
    scores = jnp.where(allowed, scores, -jnp.inf)
    shifted = jnp.exp(scores - jnp.max(scores, axis=1, keepdims=True))
    return shifted / jnp.sum(shifted, axis=1, keepdims=True)


def attend(query_side, key_side, value_side, allowed, head_count, score_scale):
    results = []
    for which_head in range(head_count):
        lower = which_head * HD
        probs = probabilities(
            query_side[:, lower : lower + HD], key_side[:, lower : lower + HD], allowed, score_scale
        )
        mixed = jnp.dot(
            probs.astype(jnp.bfloat16),
            value_side[:, lower : lower + HD],
            preferred_element_type=jnp.float32,
        )
        results.append(mixed.astype(jnp.bfloat16))
    return jnp.concatenate(results, axis=1)


def attend_back(
    query_side, key_side, value_side, allowed, attn_side, grad_side, head_count, score_scale
):
    grad_q, grad_k, grad_v = ([], [], [])
    for which_head in range(head_count):
        lower = which_head * HD
        query_head = query_side[:, lower : lower + HD]
        key_head = key_side[:, lower : lower + HD]
        value_head = value_side[:, lower : lower + HD]
        grad_head = grad_side[:, lower : lower + HD]
        attn_head = attn_side[:, lower : lower + HD]
        probs = probabilities(query_head, key_head, allowed, score_scale)
        probs_low = probs.astype(jnp.bfloat16)
        delta = jnp.sum(
            grad_head.astype(jnp.float32) * attn_head.astype(jnp.float32), axis=1, keepdims=True
        )
        dprobs = jnp.einsum("qd,kd->qk", grad_head, value_head, preferred_element_type=jnp.float32)
        dscores = (probs * (dprobs - delta)).astype(jnp.bfloat16)
        grad_q.append(
            (jnp.dot(dscores, key_head, preferred_element_type=jnp.float32) * score_scale).astype(
                jnp.bfloat16
            )
        )
        grad_k.append(
            (
                jnp.einsum("qk,qd->kd", dscores, query_head, preferred_element_type=jnp.float32)
                * score_scale
            ).astype(jnp.bfloat16)
        )
        grad_v.append(
            jnp.einsum(
                "qk,qd->kd", probs_low, grad_head, preferred_element_type=jnp.float32
            ).astype(jnp.bfloat16)
        )
    return (
        jnp.concatenate(grad_q, axis=1),
        jnp.concatenate(grad_k, axis=1),
        jnp.concatenate(grad_v, axis=1),
    )


def by_clusters(queries, key_rows, value_rows, out_weight, grad_output, cluster_ids, block_pattern):
    tokens = queries.shape[0]
    width = queries.shape[1]
    head_count = width // HD
    groups = lax.axis_size("seq")
    slot_rows = 2 * tokens // groups
    slot_total = groups * slot_rows
    blocks = block_pattern.shape[1]
    owner_index = lax.axis_index("seq")
    score_scale = 1.0 / math.sqrt(HD)
    members = (cluster_ids[:, None] == jnp.arange(groups, dtype=jnp.int32)[None, :]).astype(
        jnp.int32
    )
    earlier = jnp.cumsum(members, axis=0) - members
    local_rank = jnp.sum(earlier * members, axis=1)
    send_counts = jnp.sum(members, axis=0)
    slot_index = cluster_ids * slot_rows + local_rank

    def to_slots(row_data):
        return (
            jnp.zeros((slot_total, row_data.shape[1]), row_data.dtype).at[slot_index].set(row_data)
        )

    def from_slots(buffer):
        return jnp.take(buffer, slot_index, axis=0)

    full_weight = lax.all_gather(out_weight, "seq", axis=1, tiled=True)
    query_in, key_in, value_in, got_counts = (
        lax.all_to_all(to_slots(queries), "seq", split_axis=0, concat_axis=0, tiled=True),
        lax.all_to_all(to_slots(key_rows), "seq", split_axis=0, concat_axis=0, tiled=True),
        lax.all_to_all(to_slots(value_rows), "seq", split_axis=0, concat_axis=0, tiled=True),
        lax.all_to_all(send_counts, "seq", split_axis=0, concat_axis=0, tiled=True),
    )
    offsets = jnp.cumsum(got_counts) - got_counts
    pattern = lax.dynamic_index_in_dim(block_pattern, owner_index, 0, keepdims=False).astype(
        jnp.float32
    )
    slot_source = jnp.arange(slot_total, dtype=jnp.int32) // slot_rows
    slot_place = jnp.arange(slot_total, dtype=jnp.int32) % slot_rows
    row_live = slot_place < jnp.take(got_counts, slot_source)
    rank_rows = jnp.take(offsets, slot_source) + slot_place
    query_side, key_side, value_side = (query_in, key_in, value_in)
    onehot = (rank_rows[:, None] // BLK == jnp.arange(blocks, dtype=jnp.int32)[None, :]).astype(
        jnp.float32
    )
    block_ok = jnp.dot(jnp.dot(onehot, pattern), onehot.T) > 0.5
    usable = (
        block_ok
        & (rank_rows[None, :] <= rank_rows[:, None])
        & row_live[None, :]
        & row_live[:, None]
    )
    diagonal = jnp.eye(rank_rows.shape[0], dtype=bool)
    allowed = usable | diagonal & ~row_live[:, None]
    attn_side = attend(query_side, key_side, value_side, allowed, head_count, score_scale)
    attn_local = from_slots(
        lax.all_to_all(attn_side, "seq", split_axis=0, concat_axis=0, tiled=True)
    )
    partial_value = jnp.dot(attn_local, full_weight, preferred_element_type=jnp.float32)
    rounded_part = lax.optimization_barrier(partial_value.astype(jnp.bfloat16)).astype(jnp.float32)
    layer_out = lax.psum_scatter(
        rounded_part.astype(jnp.bfloat16), "head", scatter_dimension=1, tiled=True
    )
    grad_sum = jnp.einsum(
        "td,wd->tw",
        lax.all_gather(grad_output, "head", axis=1, tiled=True),
        full_weight,
        preferred_element_type=jnp.float32,
    )
    grad_attention = grad_sum.astype(jnp.bfloat16)
    grad_in = lax.all_to_all(
        to_slots(grad_attention), "seq", split_axis=0, concat_axis=0, tiled=True
    )
    grad_q, grad_k, grad_v = attend_back(
        query_side, key_side, value_side, allowed, attn_side, grad_in, head_count, score_scale
    )
    back_q, back_k, back_v = (
        lax.all_to_all(grad_q, "seq", split_axis=0, concat_axis=0, tiled=True),
        lax.all_to_all(grad_k, "seq", split_axis=0, concat_axis=0, tiled=True),
        lax.all_to_all(grad_v, "seq", split_axis=0, concat_axis=0, tiled=True),
    )
    return (layer_out, from_slots(back_q), from_slots(back_k), from_slots(back_v))


ID_ROWS = 16
MESH = pl.DeviceIdType.MESH


def one_hot(hit):
    return jnp.where(hit, 1.0, 0.0).astype(jnp.bfloat16)


def dot_rows(left, right):
    return lax.dot_general(
        left, right, (((1,), (0,)), ((), ())), preferred_element_type=jnp.float32
    )


def dot_last(left, right):
    return lax.dot_general(
        left, right, (((1,), (1,)), ((), ())), preferred_element_type=jnp.float32
    )


def dot_first(left, right):
    return lax.dot_general(
        left, right, (((0,), (0,)), ((), ())), preferred_element_type=jnp.float32
    )


def cluster_places(ids_ref, rows, parts, place_ref, place_cols_ref):
    before = lax.broadcasted_iota(jnp.int32, (rows, rows), 0)
    after = lax.broadcasted_iota(jnp.int32, (rows, rows), 1)
    strict = one_hot(before < after)
    names = lax.broadcasted_iota(jnp.int32, (parts, rows), 0).astype(jnp.float32)
    seen = jnp.zeros((parts, 1), jnp.float32)
    lines = []
    for part in range(parts):
        ids = jnp.concatenate(
            [
                ids_ref[part, i : i + 1, :].astype(jnp.float32)
                for i in range(rows // HD)
            ],
            axis=1,
        )
        hit = names == ids
        mark = jnp.where(hit, 1.0, 0.0)
        rank = dot_rows(mark.astype(jnp.bfloat16), strict) + seen
        lines.append(jnp.sum(mark * (rank + names * rows), axis=0, keepdims=True))
        seen = seen + jnp.sum(mark, axis=1, keepdims=True)
    places = jnp.concatenate(lines, axis=0)
    place_ref[...] = places
    padded = jnp.concatenate([places, jnp.zeros((HD - parts, rows), jnp.float32)], axis=0)
    place_cols_ref[...] = padded.T


def to_cluster(place_ref, rows, parts, cluster, read_part):
    want = lax.broadcasted_iota(jnp.int32, (rows, rows), 0).astype(jnp.float32) + (
        cluster * rows
    ).astype(jnp.float32)
    total = None
    for part in range(parts):
        pick = one_hot(want == place_ref[part : part + 1, :])
        term = dot_rows(pick, read_part(part))
        total = term if total is None else total + term
    return total.astype(jnp.bfloat16)


def from_clusters(place_cols_ref, rows, parts, part, ordered):
    lanes = lax.broadcasted_iota(jnp.int32, (rows, parts * rows), 1).astype(jnp.float32)
    pick = one_hot(place_cols_ref[:, part : part + 1] == lanes)
    return dot_rows(pick, ordered).astype(jnp.bfloat16)


def cluster_probs(pattern_ref, cluster, query, key, rows, score_scale):
    scores = dot_last(query, key) * score_scale
    row_at = lax.broadcasted_iota(jnp.int32, (rows, rows), 0)
    col_at = lax.broadcasted_iota(jnp.int32, (rows, rows), 1)
    reads = pattern_ref[cluster * 4 + 2]
    ok = (col_at <= row_at) & ((row_at // BLK == col_at // BLK) | (reads == 1))
    scores = jnp.where(ok, scores, -jnp.inf)
    shifted = jnp.exp(scores - jnp.max(scores, axis=1, keepdims=True))
    return shifted / jnp.sum(shifted, axis=1, keepdims=True)


def layer_kernel(
    rows, parts, groups, pattern_ref, ids_ref, q_ref, k_ref, v_ref, w_ref, g_ref,
    out_ref, gq_ref, gk_ref, gv_ref,
    q_in, k_in, v_in, ids_in, weight, cotangent, places, place_cols, ordered, probs_at, held,
    mixed_send, attn, grad_sum, grad_send, grad_in, dscores_at, held_qk, held_v, back_q, back_k, back_v,
    partial, shares,
    tok_send, tok_recv, ring_send, ring_recv, hop_send, hop_recv, across_send, across_recv, head_send, head_recv, own_sem,
):
    score_scale = 1.0 / math.sqrt(HD)
    me = lax.axis_index("seq")
    group = lax.axis_index("head")
    half = w_ref.shape[0] // 2
    quarter = half // 2
    ticks = parts - 1
    lower = pl.ds(half, half)
    cols = w_ref.shape[1]

    def other(j):
        return lax.rem(me + j, parts)

    def other_group(j):
        return lax.rem(group + j, groups)

    def head_at(index):
        return pl.ds(pl.multiple_of(index * HD, HD), HD)

    def along_seq(kind, j, source, target):
        return pltpu.make_async_remote_copy(
            src_ref=source, dst_ref=target, send_sem=tok_send.at[kind, j],
            recv_sem=tok_recv.at[kind, j], device_id={"seq": other(j)}, device_id_type=MESH,
        )

    def along_head(kind, j, source, target):
        return pltpu.make_async_remote_copy(
            src_ref=source, dst_ref=target, send_sem=head_send.at[kind, j],
            recv_sem=head_recv.at[kind, j], device_id={"head": other_group(j)}, device_id_type=MESH,
        )

    line = parts // 2
    row, side = me // 2, lax.rem(me, 2)
    place = row + side * (parts - 1 - 2 * row)

    def at_place(p):
        p = lax.rem(p + 2 * parts, parts)
        far = p // line
        return 2 * (p + far * (parts - 1 - 2 * p)) + far

    def ring(way, tick):
        sign = 1 - 2 * way
        block = weight.at[at_place(place - sign * tick), pl.ds(way * quarter, quarter)]
        return pltpu.make_async_remote_copy(
            src_ref=block, dst_ref=block, send_sem=ring_send.at[way, tick],
            recv_sem=ring_recv.at[way, tick], device_id={"seq": at_place(place + sign)},
            device_id_type=MESH,
        )

    def hop(way, k):
        sign = 1 - 2 * way
        block = weight.at[2 * lax.rem(row - sign * k + line, line) + side, lower]
        return pltpu.make_async_remote_copy(
            src_ref=block, dst_ref=block, send_sem=hop_send.at[way, k],
            recv_sem=hop_recv.at[way, k],
            device_id={"seq": 2 * lax.rem(row + sign + line, line) + side}, device_id_type=MESH,
        )

    def hop_goes(way, k):
        return (row >= k) & (row < line - 1) if way == 0 else (row + k < line) & (row > 0)

    def hop_comes(way, k):
        return row >= k + 1 if way == 0 else row + k + 1 < line

    def hop_owner(way, k):
        return lax.rem(row - (1 - 2 * way) * (k + 1) + line, line)

    def across(level):
        block = weight.at[2 * level + side, lower]
        return pltpu.make_async_remote_copy(
            src_ref=block, dst_ref=block, send_sem=across_send.at[level],
            recv_sem=across_recv.at[level], device_id={"seq": 2 * row + 1 - side},
            device_id_type=MESH,
        )

    own_weight = pltpu.make_async_copy(w_ref, weight.at[me], own_sem.at[0])
    own_weight.start()
    for i in range(2):
        cotangent[2 * group + i] = g_ref[:, i * cols : (i + 1) * cols]

    barrier = pltpu.get_barrier_semaphore()
    for j in range(1, parts):
        pl.semaphore_signal(barrier, inc=1, device_id={"seq": other(j)}, device_id_type=MESH)
    for j in range(1, groups):
        pl.semaphore_signal(barrier, inc=1, device_id={"head": other_group(j)}, device_id_type=MESH)
    pl.semaphore_wait(barrier, parts + groups - 2)

    own_weight.wait()
    def start_hop(way, k):
        @pl.when(hop_goes(way, k))
        def _():
            hop(way, k).start()

    for way in range(2):
        ring(way, jnp.int32(0)).start()
        start_hop(way, 0)
    across(row).start()

    def head_copies(j):
        block = cotangent.at[pl.ds(2 * group, 2)]
        return along_head(0, j, block, block)

    for j in range(1, groups):
        head_copies(j).start()

    def token_copies(j):
        dest = head_at(other(j))
        return (
            along_seq(0, j, q_ref.at[:, dest], q_in.at[me]),
            along_seq(1, j, k_ref.at[:, dest], k_in.at[me]),
            along_seq(2, j, v_ref.at[:, dest], v_in.at[me]),
            along_seq(3, j, ids_ref, ids_in.at[me]),
        )

    for j in range(1, parts):
        for copy in token_copies(j):
            copy.start()
    q_in[me] = q_ref[:, head_at(me)]
    k_in[me] = k_ref[:, head_at(me)]
    v_in[me] = v_ref[:, head_at(me)]
    ids_in[me] = ids_ref[...]

    def forward(tick):
        for way in range(2):
            ring(way, tick).wait_recv()

            @pl.when(tick + 1 < ticks)
            def _():
                ring(way, tick + 1).start()

    def accumulate(tick):
        for way in range(2):
            owner = at_place(place - (1 - 2 * way) * (tick + 1))
            here = slice(way * quarter, (way + 1) * quarter)
            grad_sum[:, here] += dot_last(cotangent[owner], weight[owner, here, :])

    def add_lower(owner):
        grad_sum[:, half:] += dot_last(cotangent[owner], weight[owner, half:, :])

    def receive_hops(k):
        for way in range(2):

            @pl.when(hop_comes(way, k))
            def _(way=way):
                hop(way, k).wait_recv()
                if k + 1 < line - 1:
                    start_hop(way, k + 1)
                across(hop_owner(way, k)).start()

        for way in range(2):

            @pl.when(hop_comes(way, k))
            def _(way=way):
                add_lower(2 * hop_owner(way, k) + side)

    def pump(tick):
        forward(jnp.int32(tick))
        accumulate(jnp.int32(tick))

    forward(jnp.int32(0))
    for j in range(1, groups):
        head_copies(j).wait()
    for i in range(4):
        lanes = slice(i * quarter, (i + 1) * quarter)
        grad_sum[:, lanes] = dot_last(cotangent[me], weight[me, lanes, :])
    accumulate(jnp.int32(0))
    pump(1)
    receive_hops(0)
    pump(2)
    for j in range(1, parts):
        for copy in token_copies(j):
            copy.wait()
    cluster_places(ids_in, rows, parts, places, place_cols)

    def read_part(part):
        return jnp.concatenate([q_in[part], k_in[part], v_in[part]], axis=1)

    def attend_cluster(cluster):
        picked = to_cluster(places, rows, parts, cluster, read_part)
        ordered[cluster] = picked
        query, key, value = (picked[:, i * HD : (i + 1) * HD] for i in range(3))
        probs = cluster_probs(pattern_ref, cluster, query, key, rows, score_scale)
        probs_at[cluster] = probs
        at = pl.multiple_of(cluster * rows, rows)
        held[pl.ds(at, rows), :] = dot_rows(probs.astype(jnp.bfloat16), value).astype(jnp.bfloat16)

    def attend_some(first, count):
        def some(cluster, _):
            attend_cluster(cluster)
            return 0

        lax.fori_loop(first, first + count, some, 0)

    share = parts // line
    for k in range(1, line - 1):
        pump(2 * k + 1)
        attend_some((2 * k - 2) * share, share)
        receive_hops(k)
        pump(2 * k + 2)
        attend_some((2 * k - 1) * share, share)
    for level in range(line):
        across(level).wait_recv()
        add_lower(2 * level + 1 - side)
    def attn_copy(j):
        return along_seq(4, j, mixed_send.at[other(j)], attn.at[:, head_at(me)])

    for part in range(parts):
        grad_send[part] = grad_sum[:, part * HD : (part + 1) * HD].astype(jnp.bfloat16)

    def grad_copy(j):
        return along_seq(5, j, grad_send.at[other(j)], grad_in.at[me])

    for j in range(1, parts):
        grad_copy(j).start()
    grad_in[me] = grad_send[me]

    for part in range(parts):
        mixed_send[part] = from_clusters(place_cols, rows, parts, part, held[...])
    for j in range(1, parts):
        attn_copy(j).start()
    attn[:, head_at(me)] = mixed_send[me]

    for j in range(1, parts):
        grad_copy(j).wait()

    def back_values(cluster, _):
        grad = to_cluster(places, rows, parts, cluster, lambda part: grad_in[part])
        value = ordered[cluster, :, 2 * HD : 3 * HD]
        probs = probs_at[cluster]
        here = pl.ds(pl.multiple_of(cluster * rows, rows), rows)
        delta = jnp.sum(
            grad.astype(jnp.float32) * held[here, :].astype(jnp.float32), axis=1, keepdims=True
        )
        dscores_at[cluster] = (probs * (dot_last(grad, value) - delta)).astype(jnp.bfloat16)
        held_v[here, :] = dot_first(probs.astype(jnp.bfloat16), grad).astype(jnp.bfloat16)
        return 0

    lax.fori_loop(0, parts, back_values, 0, unroll=2)
    for part in range(parts):
        back_v[part] = from_clusters(place_cols, rows, parts, part, held_v[...])

    def value_copy(j):
        return along_seq(6, j, back_v.at[other(j)], gv_ref.at[:, head_at(me)])

    for j in range(1, parts):
        value_copy(j).start()
    gv_ref[:, head_at(me)] = back_v[me]

    def back_scores(cluster, _):
        query, key = (ordered[cluster, :, i * HD : (i + 1) * HD] for i in range(2))
        dscores = dscores_at[cluster]
        here = pl.ds(pl.multiple_of(cluster * rows, rows), rows)
        held_qk[here, 0:HD] = (dot_rows(dscores, key) * score_scale).astype(jnp.bfloat16)
        held_qk[here, HD:] = (dot_first(dscores, query) * score_scale).astype(jnp.bfloat16)
        return 0

    lax.fori_loop(0, parts, back_scores, 0, unroll=2)
    for part in range(parts):
        back = from_clusters(place_cols, rows, parts, part, held_qk[...])
        back_q[part] = back[:, :HD]
        back_k[part] = back[:, HD:]

    def pair_copies(j):
        return (
            along_seq(7, j, back_q.at[other(j)], gq_ref.at[:, head_at(me)]),
            along_seq(8, j, back_k.at[other(j)], gk_ref.at[:, head_at(me)]),
        )

    for j in range(1, parts):
        for copy in pair_copies(j):
            copy.start()
    gq_ref[:, head_at(me)] = back_q[me]
    gk_ref[:, head_at(me)] = back_k[me]

    for j in range(1, parts):
        attn_copy(j).wait()

    def project(owner, _):
        partial[owner] = dot_rows(attn[...], weight[owner]).astype(jnp.bfloat16)
        return 0

    lax.fori_loop(0, parts, project, 0)

    def share_copy(j):
        return along_head(1, j, partial.at[pl.ds(2 * other_group(j), 2)], shares.at[group])

    for j in range(1, groups):
        share_copy(j).start()
    shares[group] = partial[pl.ds(2 * group, 2)]

    for j in range(1, groups):
        share_copy(j).wait()
    for i in range(2):
        total = shares[0, i].astype(jnp.float32)
        for j in range(1, groups):
            total = total + shares[j, i].astype(jnp.float32)
        out_ref[:, i * cols : (i + 1) * cols] = total.astype(jnp.bfloat16)

    for j in range(1, parts):
        value_copy(j).wait()
        for copy in pair_copies(j):
            copy.wait()

    def sent(tick, _):
        for way in range(2):
            ring(way, tick).wait_send()
        return 0

    lax.fori_loop(0, ticks, sent, 0)
    for k in range(line - 1):
        for way in range(2):

            @pl.when(hop_goes(way, k))
            def _(way=way, k=k):
                hop(way, k).wait_send()

    for level in range(line):
        across(level).wait_send()


VMEM_SPEC = pl.BlockSpec(memory_space=pltpu.VMEM)
SMEM_SPEC = pl.BlockSpec(memory_space=pltpu.SMEM)


def by_heads(queries, key_rows, value_rows, out_weight, grad_output, cluster_ids, block_pattern):
    rows, width = queries.shape
    parts = lax.axis_size("seq")
    groups = lax.axis_size("head")
    depth, cols = out_weight.shape
    id_rows = jnp.pad(
        cluster_ids.reshape(-1, HD).astype(jnp.bfloat16), ((0, ID_ROWS - rows // HD), (0, 0))
    )
    low, full = jnp.bfloat16, jnp.float32

    def vmem(*shape, kind=low):
        return pltpu.VMEM(shape, kind)

    scratch = [
        vmem(parts, rows, HD), vmem(parts, rows, HD), vmem(parts, rows, HD),
        vmem(parts, ID_ROWS, HD), vmem(parts, depth, cols), vmem(parts, rows, cols),
        vmem(parts, rows, kind=full), vmem(rows, HD, kind=full), vmem(parts, rows, 3 * HD),
        vmem(parts, rows, rows, kind=full), vmem(parts * rows, HD), vmem(parts, rows, HD),
        vmem(rows, width), vmem(rows, width, kind=full), vmem(parts, rows, HD),
        vmem(parts, rows, HD), vmem(parts, rows, rows), vmem(parts * rows, 2 * HD),
        vmem(parts * rows, HD), vmem(parts, rows, HD), vmem(parts, rows, HD), vmem(parts, rows, HD),
        vmem(parts, rows, cols), vmem(groups, 2, rows, cols),
        pltpu.SemaphoreType.DMA((9, parts)), pltpu.SemaphoreType.DMA((9, parts)),
        pltpu.SemaphoreType.DMA((2, parts)), pltpu.SemaphoreType.DMA((2, parts)),
        pltpu.SemaphoreType.DMA((2, parts)), pltpu.SemaphoreType.DMA((2, parts)),
        pltpu.SemaphoreType.DMA((parts,)), pltpu.SemaphoreType.DMA((parts,)),
        pltpu.SemaphoreType.DMA((2, groups)), pltpu.SemaphoreType.DMA((2, groups)),
        pltpu.SemaphoreType.DMA((1,)),
    ]
    return pl.pallas_call(
        functools.partial(layer_kernel, rows, parts, groups),
        out_shape=(jax.ShapeDtypeStruct((rows, width), low),) * 4,
        in_specs=[SMEM_SPEC] + [VMEM_SPEC] * 6,
        out_specs=(VMEM_SPEC,) * 4,
        scratch_shapes=scratch,
        compiler_params=pltpu.CompilerParams(
            collective_id=0, has_side_effects=True, vmem_limit_bytes=56 * 1024 * 1024
        ),
        name="routing_layer",
    )(block_pattern.reshape(-1), id_rows, queries, key_rows, value_rows, out_weight, grad_output)


def on_device(queries, *others):
    heads = queries.shape[1] // HD
    parts, groups = lax.axis_size("seq"), lax.axis_size("head")
    if heads == parts == 2 * groups and others[-1].shape[1] == 2:
        return by_heads(queries, *others)
    return by_clusters(queries, *others)


def solution(mesh):
    in_specs = (
        P("seq", "head"),
        P("seq", "head"),
        P("seq", "head"),
        P("head", "seq"),
        P("seq", "head"),
        P("seq"),
        P(),
    )
    out_specs = (P("seq", "head"), P("seq", "head"), P("seq", "head"), P("seq", "head"))
    return jax.shard_map(
        on_device, mesh=mesh, in_specs=in_specs, out_specs=out_specs, check_vma=False
    )
```
